256 devices in a mesh: row: 32 (over y, x, core), col: 8 (over z).
Axes of the slice: x: 4, y: 4, z: 8, core: 2. Of those that a mesh axis runs over, the one named last changes fastest.
Arguments:
- alignment_matrix: bfloat16 [128, 2048, 256], P(None, ('row', 'col')), may hold values from -70 to 70, as said below
- standardize_factor: float32 [256], replicated, may hold values from 0.4 to 1.6
- standardize_shift: float32 [256], replicated, may hold values from -3 to 3
- first_map_matrix: bfloat16 [256, 32], replicated, may hold values from -0.375 to 0.375
- first_map_offset: float32 [32], replicated, may hold values from -3 to 3
- second_map_matrix: bfloat16 [256, 32], replicated, may hold values from -0.375 to 0.375
- second_map_offset: float32 [32], replicated, may hold values from -3 to 3
- couple_map_matrix: bfloat16 [1024, 128], replicated, may hold values from -1.5 to 1.5
- couple_map_offset: float32 [128], replicated, may hold values from -3 to 3
Outputs:
- pair_update: bfloat16 [2048, 2048, 128], P(('row', 'col'))
The draws below stay inside these ranges and needn't reach their ends.
Inputs may be any that keep to these rules, and one draw needn't show every extreme that they name: `alignment_matrix`: MSA features.
All inputs are finite; a program needn't handle non-finite values.
Results may differ from the reference program's by a relative error of at most 0.0051.
Values may be sent and summed in bfloat16 or wider, within the bound.
No kernel may reach another device: no remote copies, remote signals or barrier semaphores. Data moves between devices by JAX's collectives and lax.ppermute only.
A program may use at most 128 MiB of HBM per device.

```python
import math
import jax
import jax.numpy as jnp
from jax import lax

CM = 256
CH = 32
CZ = 128
S = 128
R = 2048


def draw_alignment_matrix(key, part):
    key = jax.random.fold_in(key, 11)
    base_key, row_key, chan_key = jax.random.split(key, 3)
    base = jnp.clip(jax.random.normal(base_key, (S, R, CM), jnp.float32), -4.0, 4.0)
    row_scale = jnp.exp(jax.random.uniform(row_key, (S, R, 1), jnp.float32, 0.0, math.log(10.0)))
    chan_scale = jnp.exp(jax.random.uniform(chan_key, (CM,), jnp.float32, -0.5, 0.5))
    return (base * row_scale * chan_scale).astype(jnp.bfloat16)


def noise(own_key, extent, spread, bound, kind=jnp.bfloat16):
    entries = jax.random.normal(own_key, extent, jnp.float32) * spread
    return jnp.minimum(jnp.maximum(entries, -bound), bound).astype(kind)


def setup_inputs(seed: int = 0) -> dict:
    keys = jax.random.split(jax.random.key(seed), 10)
    return {
        "alignment_matrix": draw_alignment_matrix(jax.random.fold_in(keys[9], 71), 0),
        "standardize_factor": jnp.clip(1.0 + 0.12 * jax.random.normal(keys[1], (CM,), jnp.float32), 0.4, 1.6),
        "standardize_shift": noise(keys[2], (CM,), 0.5, 3.0, jnp.float32),
        "first_map_matrix": noise(keys[3], (CM, CH), CM ** -0.5, 0.375),
        "first_map_offset": noise(keys[4], (CH,), 0.5, 3.0, jnp.float32),
        "second_map_matrix": noise(keys[5], (CM, CH), CM ** -0.5, 0.375),
        "second_map_offset": noise(keys[6], (CH,), 0.5, 3.0, jnp.float32),
        "couple_map_matrix": noise(keys[7], (CH * CH, CZ), 16 ** -0.5, 1.5),
        "couple_map_offset": noise(keys[8], (CZ,), 0.5, 3.0, jnp.float32),
    }


def standardize_rows(alignment_matrix, standardize_factor, standardize_shift):
    element_list = alignment_matrix.astype(jnp.float32)
    mean = lax.optimization_barrier(jnp.mean(element_list, axis=-1, keepdims=True))
    centered = element_list - mean
    variance = lax.optimization_barrier(jnp.mean(centered * centered, axis=-1, keepdims=True))
    return (centered * lax.rsqrt(variance + 1e-05) * standardize_factor + standardize_shift).astype(jnp.bfloat16)

def project(standardized_alignment, weight, bias):
    return (jnp.einsum('srm,mc->src', standardized_alignment.astype(jnp.float32), weight.astype(jnp.float32)) + bias).astype(jnp.bfloat16)

def reference(alignment_matrix, standardize_factor, standardize_shift, first_map_matrix, first_map_offset, second_map_matrix, second_map_offset, couple_map_matrix, couple_map_offset):
    standardized_alignment = standardize_rows(alignment_matrix, standardize_factor, standardize_shift)
    left = project(standardized_alignment, first_map_matrix, first_map_offset)
    right = project(standardized_alignment, second_map_matrix, second_map_offset)
    right_f = right.astype(jnp.float32)
    weight_f = couple_map_matrix.astype(jnp.float32)
    blocks = left.reshape(S, R // 8 if R % 8 == 0 else R, -1, CH) if False else None
    step_rows = 8 if R % 8 == 0 else 1
    left_blocks = jnp.moveaxis(left.astype(jnp.float32).reshape(S, R // step_rows, step_rows, CH), 1, 0)

    def one_block(left_part):
        outer = jnp.einsum('sic,sje->ijce', left_part, right_f) / S
        outer = outer.astype(jnp.bfloat16).astype(jnp.float32).reshape(step_rows, R, CH * CH)
        return (jnp.einsum('ijk,kf->ijf', outer, weight_f) + couple_map_offset).astype(jnp.bfloat16)
    result = lax.map(one_block, left_blocks)
    return result.reshape(R, R, CZ)
```

```python
import functools

import jax
import jax.numpy as jnp
from jax import lax
from jax.experimental import pallas as pl
from jax.experimental.pallas import tpu as pltpu
from jax.sharding import Mesh, PartitionSpec as P

SIZES = {"y": 4, "x": 4, "c": 2, "z": 8}
S, CM, CH, CZ, LOCAL, UNITS = 128, 256, 32, 128, 8, 128
PARTS = ((0, 12), (12, 22), (22, 32))
VMEM_LIMIT = 56 * 1024 * 1024


def project_kernel(msa_ref, gain_ref, shift_ref, w1_ref, b1_ref, w2_ref, b2_ref, ra_ref, rb_ref, rc_ref, lt_ref,
                   w_s, y_s, r_s):
    x = msa_ref[...].astype(jnp.float32).reshape(S * LOCAL, CM)
    mean = jnp.mean(x, axis=-1, keepdims=True)
    centered = x - mean
    variance = jnp.mean(centered * centered, axis=-1, keepdims=True)
    normed = (centered * lax.rsqrt(variance + 1e-05) * gain_ref[...] + shift_ref[...]).astype(jnp.bfloat16)
    w_s[:, 0:CH] = w1_ref[...]
    w_s[:, CH:2 * CH] = w2_ref[...]
    y = jnp.dot(normed, w_s[...], preferred_element_type=jnp.float32)
    bias = jnp.concatenate([b1_ref[...], b2_ref[...]], axis=1)
    y_s[:, 0:2 * CH] = (y + bias).astype(jnp.bfloat16).astype(jnp.float32)
    for j in range(LOCAL):
        t = y_s[pl.ds(j, S, stride=LOCAL), :].T
        lt_ref[j * CH:(j + 1) * CH, :] = t[0:CH].astype(jnp.bfloat16)
        r_s[j * CH:(j + 1) * CH, :] = t[CH:2 * CH]
    for (lo, hi), ref in zip(PARTS, (ra_ref, rb_ref, rc_ref)):
        for e in range(lo, hi):
            ref[:, (e - lo) * S:(e - lo + 1) * S] = r_s[pl.ds(e, LOCAL, stride=CH), :].astype(jnp.bfloat16)


def project(msa, gain, shift, w1, b1, w2, b2):
    widths = [(hi - lo) * S for lo, hi in PARTS]
    return pl.pallas_call(
        project_kernel,
        out_shape=[jax.ShapeDtypeStruct((LOCAL, k), jnp.bfloat16) for k in widths]
        + [jax.ShapeDtypeStruct((LOCAL * CH, S), jnp.bfloat16)],
        scratch_shapes=[
            pltpu.VMEM((CM, 2 * CH), jnp.bfloat16),
            pltpu.VMEM((S * LOCAL, S), jnp.float32),
            pltpu.VMEM((LOCAL * CH, S), jnp.float32),
        ],
        compiler_params=pltpu.CompilerParams(vmem_limit_bytes=VMEM_LIMIT),
        name="project",
    )(msa, gain.reshape(1, CM), shift.reshape(1, CM), w1, b1.reshape(1, CH), w2, b2.reshape(1, CH))


def couple_kernel(lt_ref, w_ref, t_ref):
    for i in range(2):
        t = lax.dot_general(lt_ref[i * CH:(i + 1) * CH, :], w_ref[...], (((0,), (0,)), ((), ())),
                            preferred_element_type=jnp.float32)
        t = (t * (1.0 / S)).astype(jnp.bfloat16)
        for e in range(CH):
            t_ref[0, e * S:(e + 1) * S, i * CZ:(i + 1) * CZ] = t[:, e * CZ:(e + 1) * CZ]


def couple(lt, w):
    return pl.pallas_call(
        couple_kernel,
        grid=(LOCAL // 2,),
        in_specs=[
            pl.BlockSpec((2 * CH, S), lambda n: (n, 0)),
            pl.BlockSpec((CH, CH * CZ), lambda n: (0, 0)),
        ],
        out_specs=pl.BlockSpec((1, CH * S, 2 * CZ), lambda n: (n, 0, 0)),
        out_shape=jax.ShapeDtypeStruct((LOCAL // 2, CH * S, 2 * CZ), jnp.bfloat16),
        compiler_params=pltpu.CompilerParams(vmem_limit_bytes=VMEM_LIMIT),
        cost_estimate=pl.CostEstimate(flops=2 * LOCAL * S * CH * CH * CZ, bytes_accessed=8 << 20, transcendentals=0),
        name="couple",
    )(lt, w)


def place4(own, core, t):
    rel = jnp.where((own + core) % 2 == 0, t - own, own - t) & 3
    return rel ^ (rel >> 1)


def place8(own, core, t):
    rel = jnp.where((own + core) % 2 == 0, t - own, own - t) & 7
    half, low = rel >> 1, rel & 1
    return jnp.where(half == 0, low, jnp.where(half == 1, 4 + low, jnp.where(half == 2, 7 - low, 3 - low)))


def pair_kernel(at_ref, ra_ref, rb_ref, rc_ref, t_ref, bias_ref, o_ref, sa, sb, sc):
    for (lo, hi), r_ref, s_ref in zip(PARTS, (ra_ref, rb_ref, rc_ref), (sa, sb, sc)):
        s_ref[...] = jnp.dot(r_ref[...], t_ref[0, lo * S:hi * S, :], preferred_element_type=jnp.float32)
    c, y, x, z = at_ref[0], at_ref[1], at_ref[2], at_ref[3]
    bias = jnp.concatenate([bias_ref[...], bias_ref[...]], axis=1)
    px = [place4(x, c, t) for t in range(4)]
    py = [place4(y, c, t) for t in range(4)]
    pz = [place8(z, c, t) for t in range(8)]

    def rows(ref, unit):
        return ref[pl.ds(pl.multiple_of(unit * LOCAL, LOCAL), LOCAL), :]

    for ty in range(4):
        for tx in range(4):
            for tz in range(8):
                value = (
                    rows(sa, (tz * 4 + py[ty]) * 4 + px[tx])
                    + rows(sb, (px[tx] * 8 + pz[tz]) * 4 + py[ty])
                    + rows(sc, (py[ty] * 4 + px[tx]) * 8 + pz[tz])
                    + bias
                ).astype(jnp.bfloat16)
                for i in range(2):
                    o_ref[i, ty * 4 + tx, 0, tz * LOCAL:(tz + 1) * LOCAL, :] = value[:, i * CZ:(i + 1) * CZ]


def pair(at, ra, rb, rc, t, bias, whole):
    widths = [(hi - lo) * S for lo, hi in PARTS]
    return pl.pallas_call(
        pair_kernel,
        grid_spec=pltpu.PrefetchScalarGridSpec(
            num_scalar_prefetch=1,
            grid=(LOCAL // 2,),
            in_specs=[pl.BlockSpec((UNITS * LOCAL, k), lambda n, at: (0, 0)) for k in widths]
            + [
                pl.BlockSpec((1, CH * S, 2 * CZ), lambda n, at: (n, 0, 0)),
                pl.BlockSpec((1, CZ), lambda n, at: (0, 0)),
            ],
            out_specs=pl.BlockSpec((2, 16, 1, 64, CZ), lambda n, at: (n, 0, at[0] if whole else 0, 0, 0)),
            scratch_shapes=[pltpu.VMEM((UNITS * LOCAL, 2 * CZ), jnp.float32)] * 3,
        ),
        out_shape=jax.ShapeDtypeStruct((LOCAL, 16, 2 if whole else 1, 64, CZ), jnp.bfloat16),
        compiler_params=pltpu.CompilerParams(vmem_limit_bytes=VMEM_LIMIT),
        cost_estimate=pl.CostEstimate(flops=2 * 1024 * 4096 * 1024, bytes_accessed=16 << 20, transcendentals=0),
        name="pair",
    )(at, ra, rb, rc, t, bias.reshape(1, CZ))


def exchange(v, axis, step):
    n, pairs = SIZES[axis], []
    for core in range(2):
        even_up = (step % 2 == 0) == (core == 0)
        for i in range(n):
            partner = (i + 1 if (i % 2 == 0) == even_up else i - 1) % n
            flat = (lambda k: core * n + k) if axis == "z" else (lambda k: k * 2 + core)
            pairs.append((flat(i), flat(partner)))
    return lax.ppermute(v, ("c", "z") if axis == "z" else (axis, "c"), pairs)


def gather(v, axis):
    first = exchange(v, axis, 0)
    held = [jnp.concatenate([v, first], axis=0)]
    for step in range(1, SIZES[axis] // 2):
        held.append(exchange(held[-1], axis, step))
    return jnp.concatenate(held, axis=0)


def gather_last(v, axis):
    first = exchange(v, axis, 0)
    second = exchange(v, axis, 1)
    third = exchange(first, axis, 1)
    return jnp.concatenate([v, first, second, third], axis=0)


def per_device(msa, gain, shift, w1, b1, w2, b2, couple_map, couple_offset):
    core = lax.axis_index("c")
    at = jnp.stack([core, lax.axis_index("y"), lax.axis_index("x"), lax.axis_index("z")]).astype(jnp.int32)
    ra, rb, rc, lt = project(msa, gain, shift, w1, b1, w2, b2)
    other = [(0, 1), (1, 0)]
    lt_other = lax.ppermute(lt, "c", other)
    w = couple_map.reshape(CH, CH * CZ)

    ra = gather(gather(ra, "x"), "y")
    rb = gather(gather(rb, "y"), "z")
    rc = gather(gather(rc, "z"), "x")
    ra = lax.all_gather(ra, "z", axis=0, tiled=True)
    rb = gather_last(rb, "x")
    rc = gather_last(rc, "y")

    theirs = pair(at, ra, rb, rc, couple(lt_other, w), couple_offset, False)
    got = lax.ppermute(theirs, "c", other)
    mine = pair(at, ra, rb, rc, couple(lt, w), couple_offset, True)
    out = lax.dynamic_update_slice(mine, got, (0, 0, 1 - core, 0, 0))
    return out.reshape(LOCAL, 16 * 2 * 64, CZ)


def solution(mesh):
    fine = Mesh(mesh.devices.reshape(4, 4, 2, 8), ("y", "x", "c", "z"))
    rows = ("y", "x", "c", "z")
    return jax.shard_map(
        per_device,
        mesh=fine,
        in_specs=(P(None, rows, None), P(), P(), P(), P(), P(), P(), P(), P()),
        out_specs=P(rows, None, None),
        check_vma=False,
    )
```

```python
import jax
import jax.numpy as jnp
from jax import lax
from jax.experimental import pallas as pl
from jax.experimental.pallas import tpu as pltpu
from jax.sharding import Mesh, PartitionSpec as P

S, CM, CH, CZ, LOCAL = 128, 256, 32, 128, 8
EH = CH // 2
HALF = EH * S
UNIT = 2 * LOCAL
BLOCK = 4 * 8 * UNIT
MIB = 1024 * 1024
BF16, F32 = jnp.bfloat16, jnp.float32


def project_kernel(core_ref, msa_in, gain_in, shift_in, w1_in, b1_in, w2_in, b2_in, keep_ref, give_ref, lt_ref,
                   msa_ref, gain_ref, shift_ref, w_s, b1_ref, b2_ref, y_s, r_s, sem):
    pairs = ((msa_in, msa_ref), (gain_in, gain_ref), (shift_in, shift_ref), (w1_in, w_s.at[pl.ds(0, CH)]),
             (w2_in, w_s.at[pl.ds(CH, CH)]), (b1_in, b1_ref), (b2_in, b2_ref))
    copies = [pltpu.make_async_copy(src, dst, sem.at[k]) for k, (src, dst) in enumerate(pairs)]
    for copy in copies:
        copy.start()
    for copy in copies:
        copy.wait()
    x = msa_ref[...].astype(F32).reshape(S * LOCAL, CM)
    mean = jnp.mean(x, axis=-1, keepdims=True)
    centered = x - mean
    variance = jnp.mean(centered * centered, axis=-1, keepdims=True)
    normed = (centered * lax.rsqrt(variance + 1e-05) * gain_ref[...] + shift_ref[...]).astype(BF16)
    y = lax.dot_general(normed, w_s[...], (((1,), (1,)), ((), ())), preferred_element_type=F32)
    bias = jnp.concatenate([b1_ref[...], b2_ref[...]], axis=1)
    y_s[:, 0:2 * CH] = (y + bias).astype(BF16).astype(F32)
    for j in range(LOCAL):
        t = y_s[pl.ds(j, S, stride=LOCAL), :].T
        lt_ref[j * CH:(j + 1) * CH, :] = (t[0:CH] * (1.0 / S)).astype(BF16)
        r_s[j * CH:(j + 1) * CH, :] = t[CH:2 * CH]
    core = core_ref[0]
    for e in range(EH):
        keep_ref[:, e * S:(e + 1) * S] = r_s[pl.ds(core * EH + e, LOCAL, stride=CH), :].astype(BF16)
        give_ref[:, e * S:(e + 1) * S] = r_s[pl.ds((1 - core) * EH + e, LOCAL, stride=CH), :].astype(BF16)


def project(core, msa, gain, shift, w1, b1, w2, b2):
    return pl.pallas_call(
        project_kernel,
        grid_spec=pltpu.PrefetchScalarGridSpec(
            num_scalar_prefetch=1,
            grid=(1,),
            in_specs=[pl.BlockSpec(memory_space=pl.ANY)] * 7,
            out_specs=[
                pl.BlockSpec((LOCAL, HALF), lambda n, core: (0, 0)),
                pl.BlockSpec((LOCAL, HALF), lambda n, core: (0, 0)),
                pl.BlockSpec((LOCAL * CH, S), lambda n, core: (0, 0)),
            ],
            scratch_shapes=[
                pltpu.VMEM((S, LOCAL, CM), BF16),
                pltpu.VMEM((1, CM), F32),
                pltpu.VMEM((1, CM), F32),
                pltpu.VMEM((2 * CH, CM), BF16),
                pltpu.VMEM((1, CH), F32),
                pltpu.VMEM((1, CH), F32),
                pltpu.VMEM((S * LOCAL, S), F32),
                pltpu.VMEM((LOCAL * CH, S), F32),
                pltpu.SemaphoreType.DMA((7,)),
            ],
        ),
        out_shape=[
            jax.ShapeDtypeStruct((LOCAL, HALF), BF16),
            jax.ShapeDtypeStruct((LOCAL, HALF), BF16),
            jax.ShapeDtypeStruct((LOCAL * CH, S), BF16),
        ],
        compiler_params=pltpu.CompilerParams(vmem_limit_bytes=60 * MIB),
        name="project",
    )(core, msa, gain.reshape(1, CM), shift.reshape(1, CM), w1.T, b1.reshape(1, CH), w2.T, b2.reshape(1, CH))


def couple_kernel(theirs_ref, mine_ref, w_ref, t_ref):
    lt = jnp.where(pl.program_id(0) < 2, theirs_ref[...], mine_ref[...])
    for n in range(2):
        for i in range(2):
            row = (n * 2 + i) * CH
            t = lax.dot_general(lt[row:row + CH, :], w_ref[...], (((0,), (0,)), ((), ())),
                                preferred_element_type=F32).astype(BF16)
            for e in range(EH):
                t_ref[n, e * S:(e + 1) * S, i * CZ:(i + 1) * CZ] = t[:, e * CZ:(e + 1) * CZ]


def couple(theirs, mine, w):
    return pl.pallas_call(
        couple_kernel,
        grid=(4,),
        in_specs=[
            pl.BlockSpec((4 * CH, S), lambda n: (n % 2, 0)),
            pl.BlockSpec((4 * CH, S), lambda n: (n % 2, 0)),
            pl.BlockSpec((CH, EH * CZ), lambda n: (0, 0)),
        ],
        out_specs=pl.BlockSpec((2, HALF, 2 * CZ), lambda n: (n, 0, 0)),
        out_shape=jax.ShapeDtypeStruct((LOCAL, HALF, 2 * CZ), BF16),
        compiler_params=pltpu.CompilerParams(vmem_limit_bytes=16 * MIB),
        cost_estimate=pl.CostEstimate(flops=2 * 16 * S * CH * EH * CZ, bytes_accessed=9 * MIB, transcendentals=0),
        name="couple",
    )(theirs, mine, w)


def place8(own, core, t):
    rel = jnp.where((own + core) % 2 == 0, t - own, own - t) & 7
    half, low = rel >> 1, rel & 1
    return jnp.where(half == 0, low, jnp.where(half == 1, 4 + low, jnp.where(half == 2, 7 - low, 3 - low)))


def place4(own, core, t):
    rel = jnp.where((own + core) % 2 == 0, t - own, own - t) & 3
    return rel ^ (rel >> 1)


def holder4(own, core, k):
    step = (0, 1, -1, -2)[k]
    return (own + jnp.where((own + core) % 2 == 0, step, -step)) & 3


def block_kernel(count, at_ref, *refs):
    r_refs, t_ref, o_refs, sum_s = refs[:count], refs[count], refs[count + 1:-1], refs[-1]
    core, z = at_ref[0], at_ref[3]
    minor = jnp.where(core == 0, at_ref[1], at_ref[2])
    pm = [place4(minor, core, t) for t in range(4)]
    pz = [place8(z, core, t) for t in range(8)]
    rows = BLOCK // count
    for n in range(2):
        for k in range(count):
            sum_s[n, k * rows:(k + 1) * rows, :] = jnp.dot(r_refs[k][...], t_ref[n], preferred_element_type=F32)

    def store(o_ref):
        for n in range(2):
            for tm in range(4):
                for c in range(2):
                    side = jnp.where(core == c, 0, LOCAL)
                    for tz in range(0, 8, 2):
                        both = [
                            sum_s[n, pl.ds(pl.multiple_of((pm[tm] * 8 + pz[tz + d]) * UNIT + side, LOCAL), LOCAL), :]
                            for d in range(2)
                        ]
                        value = jnp.concatenate(both, axis=0).astype(BF16)
                        for i in range(2):
                            o_ref[n * 2 + i, tm, c, tz * LOCAL:(tz + 2) * LOCAL, :] = value[:, i * CZ:(i + 1) * CZ]

    if len(o_refs) == 1:
        store(o_refs[0])
    else:
        pl.when(pl.program_id(0) < 2)(lambda: store(o_refs[0]))
        pl.when(pl.program_id(0) >= 2)(lambda: store(o_refs[1]))


def block(at, pieces, t, part):
    count = len(pieces)
    rows = BLOCK // count
    first = 2 if part == 1 else 0
    shape = (LOCAL, 4, 2, 64, CZ)
    spec = lambda where: pl.BlockSpec((4,) + shape[1:], lambda n, at: (where(n), 0, 0, 0, 0))
    if part is None:
        out_specs = [spec(lambda n: jnp.minimum(n, 1)), spec(lambda n: jnp.maximum(n - 2, 0))]
    else:
        out_specs = [spec(lambda n: n)]
    return pl.pallas_call(
        lambda *refs: block_kernel(count, *refs),
        grid_spec=pltpu.PrefetchScalarGridSpec(
            num_scalar_prefetch=1,
            grid=(4 if part is None else 2,),
            in_specs=[pl.BlockSpec((rows, HALF), lambda n, at: (0, 0))] * count
            + [pl.BlockSpec((2, HALF, 2 * CZ), lambda n, at: (first + n, 0, 0))],
            out_specs=out_specs,
            scratch_shapes=[pltpu.VMEM((2, BLOCK, 2 * CZ), F32)],
        ),
        out_shape=[jax.ShapeDtypeStruct(shape, BF16)] * len(out_specs),
        compiler_params=pltpu.CompilerParams(vmem_limit_bytes=24 * MIB),
        cost_estimate=pl.CostEstimate(flops=2 * BLOCK * HALF * 1024 * len(out_specs), bytes_accessed=10 * MIB,
                                      transcendentals=0),
        name="block",
    )(at, *pieces, t)


def add_kernel(at_ref, *refs):
    mine, theirs, bias_ref, o_ref = refs[0:4], refs[4:8], refs[8], refs[9]
    core = at_ref[0]
    minor = jnp.where(core == 0, at_ref[1], at_ref[2])
    major = jnp.where(core == 0, at_ref[2], at_ref[1])
    bias = bias_ref[...]
    for k in range(4):
        a = holder4(major, core, k)
        for m in range(4):
            b = holder4(minor, 1 - core, m)
            group = jnp.where(core == 0, b * 4 + a, a * 4 + b)
            for i in range(2):
                v = mine[k][i, b].astype(F32) + theirs[m][i, a].astype(F32)
                o_ref[i, group] = (v.reshape(128, CZ) + bias).astype(BF16).reshape(2, 64, CZ)


def add(at, mine, theirs, bias):
    return pl.pallas_call(
        add_kernel,
        grid_spec=pltpu.PrefetchScalarGridSpec(
            num_scalar_prefetch=1,
            grid=(LOCAL // 2,),
            in_specs=[pl.BlockSpec((2, 4, 2, 64, CZ), lambda n, at: (n, 0, 0, 0, 0))] * 8
            + [pl.BlockSpec((1, CZ), lambda n, at: (0, 0))],
            out_specs=pl.BlockSpec((2, 16, 2, 64, CZ), lambda n, at: (n, 0, 0, 0, 0)),
        ),
        out_shape=jax.ShapeDtypeStruct((LOCAL, 16, 2, 64, CZ), BF16),
        compiler_params=pltpu.CompilerParams(vmem_limit_bytes=24 * MIB),
        cost_estimate=pl.CostEstimate(flops=10**7, bytes_accessed=13 * MIB, transcendentals=0),
        name="add",
    )(at, *mine, *theirs, bias.reshape(1, CZ))


def partner(k, n, core, step):
    return (k + 1 if (k + core + step) % 2 == 0 else k - 1) % n


def along_z(v, step):
    return lax.ppermute(
        v, ("c", "z"), [(c * 8 + k, c * 8 + partner(k, 8, c, step)) for c in range(2) for k in range(8)])


def along_plane(v, last, step):
    pairs = []
    for y in range(4):
        for x in range(4):
            for c in range(2):
                ny, nx = (y, partner(x, 4, c, step)) if (c == 0) == last else (partner(y, 4, c, step), x)
                pairs.append(((y * 4 + x) * 2 + c, (ny * 4 + nx) * 2 + c))
    return lax.ppermute(v, ("y", "x", "c"), pairs)


def swap(v):
    return lax.ppermute(v, "c", [(0, 1), (1, 0)])


def join(*blocks):
    return jnp.concatenate(blocks, axis=0)


def together(*values):
    return lax.optimization_barrier(values)


def per_device(msa, gain, shift, w1, b1, w2, b2, couple_map, couple_offset):
    core = lax.axis_index("c")
    at = jnp.stack([core, lax.axis_index("y"), lax.axis_index("x"), lax.axis_index("z")]).astype(jnp.int32)
    keep, give, lt = project(at, msa, gain, shift, w1, b1, w2, b2)
    r = join(keep, swap(give))
    lt_sibling = swap(lt)
    w = lax.dynamic_slice_in_dim(couple_map.reshape(CH, CH, CZ), core * EH, EH, axis=1).reshape(CH, EH * CZ)

    z1 = join(r, along_z(r, 0))
    z2 = along_z(z1, 1)
    z3 = along_z(z2, 2)
    z4 = along_z(z3, 3)
    r = join(z1, z2, z3, z4)

    m1 = along_plane(r, False, 0)
    m2 = along_plane(r, False, 1)
    m3 = along_plane(m1, False, 1)
    t = couple(lt_sibling, lt, w)
    b0 = join(r, m1, m2, m3)

    b1 = along_plane(b0, True, 0)
    b2 = along_plane(b0, True, 1)
    p0, q0 = block(at, [b0], t, None)
    b1, b2, p0, q0 = together(b1, b2, p0, q0)
    b3 = along_plane(b1[:BLOCK // 2], True, 1), along_plane(b2[BLOCK // 2:], True, 0)
    p1, q1 = block(at, [b1], t, None)
    p2, q2 = block(at, [b2], t, None)
    p3, = block(at, b3, t, 0)
    q3, = block(at, b3, t, 1)
    theirs = [swap(p) for p in (p0, p1, p2, p3)]
    mine = [q0, q1, q2, q3]
    return add(at, mine, theirs, couple_offset).reshape(LOCAL, 16 * 2 * 64, CZ)


def solution(mesh):
    fine = Mesh(mesh.devices.reshape(4, 4, 2, 8), ("y", "x", "c", "z"))
    rows = ("y", "x", "c", "z")
    return jax.shard_map(
        per_device,
        mesh=fine,
        in_specs=(P(None, rows, None), P(), P(), P(), P(), P(), P(), P(), P()),
        out_specs=P(rows, None, None),
        check_vma=False,
    )
```

```python
import jax
import jax.numpy as jnp
from jax import lax
from jax.experimental import pallas as pl
from jax.experimental.pallas import tpu as pltpu
from jax.sharding import Mesh, PartitionSpec as P

S, CM, CH, CZ, LOCAL = 128, 256, 32, 128, 8
EH = CH // 2
HALF = EH * S
UNIT = 2 * LOCAL
BLOCK = 4 * 8 * UNIT
MIB = 1024 * 1024
BF16, F32 = jnp.bfloat16, jnp.float32


def project_kernel(core_ref, msa_in, gain_in, shift_in, w1_in, b1_in, w2_in, b2_in, keep_ref, give_ref, lt_ref,
                   msa_ref, gain_ref, shift_ref, w_s, b1_ref, b2_ref, y_s, r_s, sem):
    pairs = ((msa_in, msa_ref), (gain_in, gain_ref), (shift_in, shift_ref), (w1_in, w_s.at[pl.ds(0, CH)]),
             (w2_in, w_s.at[pl.ds(CH, CH)]), (b1_in, b1_ref), (b2_in, b2_ref))
    copies = [pltpu.make_async_copy(src, dst, sem.at[k]) for k, (src, dst) in enumerate(pairs)]
    for copy in copies:
        copy.start()
    for copy in copies:
        copy.wait()
    x = msa_ref[...].astype(F32).reshape(S * LOCAL, CM)
    mean = jnp.mean(x, axis=-1, keepdims=True)
    centered = x - mean
    variance = jnp.mean(centered * centered, axis=-1, keepdims=True)
    normed = (centered * lax.rsqrt(variance + 1e-05) * gain_ref[...] + shift_ref[...]).astype(BF16)
    y = lax.dot_general(normed, w_s[...], (((1,), (1,)), ((), ())), preferred_element_type=F32)
    bias = jnp.concatenate([b1_ref[...], b2_ref[...]], axis=1)
    y_s[:, 0:2 * CH] = (y + bias).astype(BF16).astype(F32)
    for j in range(LOCAL):
        t = y_s[pl.ds(j, S, stride=LOCAL), :].T
        lt_ref[j * CH:(j + 1) * CH, :] = (t[0:CH] * (1.0 / S)).astype(BF16)
        r_s[j * CH:(j + 1) * CH, :] = t[CH:2 * CH]
    core = core_ref[0]
    for e in range(EH):
        keep_ref[:, e * S:(e + 1) * S] = r_s[pl.ds(core * EH + e, LOCAL, stride=CH), :].astype(BF16)
        give_ref[:, e * S:(e + 1) * S] = r_s[pl.ds((1 - core) * EH + e, LOCAL, stride=CH), :].astype(BF16)


def project(core, msa, gain, shift, w1, b1, w2, b2):
    return pl.pallas_call(
        project_kernel,
        grid_spec=pltpu.PrefetchScalarGridSpec(
            num_scalar_prefetch=1,
            grid=(1,),
            in_specs=[pl.BlockSpec(memory_space=pl.ANY)] * 7,
            out_specs=[
                pl.BlockSpec((LOCAL, HALF), lambda n, core: (0, 0)),
                pl.BlockSpec((LOCAL, HALF), lambda n, core: (0, 0)),
                pl.BlockSpec((LOCAL * CH, S), lambda n, core: (0, 0)),
            ],
            scratch_shapes=[
                pltpu.VMEM((S, LOCAL, CM), BF16),
                pltpu.VMEM((1, CM), F32),
                pltpu.VMEM((1, CM), F32),
                pltpu.VMEM((2 * CH, CM), BF16),
                pltpu.VMEM((1, CH), F32),
                pltpu.VMEM((1, CH), F32),
                pltpu.VMEM((S * LOCAL, S), F32),
                pltpu.VMEM((LOCAL * CH, S), F32),
                pltpu.SemaphoreType.DMA((7,)),
            ],
        ),
        out_shape=[
            jax.ShapeDtypeStruct((LOCAL, HALF), BF16),
            jax.ShapeDtypeStruct((LOCAL, HALF), BF16),
            jax.ShapeDtypeStruct((LOCAL * CH, S), BF16),
        ],
        compiler_params=pltpu.CompilerParams(vmem_limit_bytes=60 * MIB),
        name="project",
    )(core, msa, gain.reshape(1, CM), shift.reshape(1, CM), w1.T, b1.reshape(1, CH), w2.T, b2.reshape(1, CH))


def couple_kernel(theirs_ref, mine_ref, w_ref, t_ref):
    lt = jnp.where(pl.program_id(0) < 2, theirs_ref[...], mine_ref[...])
    for n in range(2):
        for i in range(2):
            row = (n * 2 + i) * CH
            t = lax.dot_general(lt[row:row + CH, :], w_ref[...], (((0,), (0,)), ((), ())),
                                preferred_element_type=F32).astype(BF16)
            for e in range(EH):
                t_ref[n, e * S:(e + 1) * S, i * CZ:(i + 1) * CZ] = t[:, e * CZ:(e + 1) * CZ]


def couple(theirs, mine, w):
    return pl.pallas_call(
        couple_kernel,
        grid=(4,),
        in_specs=[
            pl.BlockSpec((4 * CH, S), lambda n: (n % 2, 0)),
            pl.BlockSpec((4 * CH, S), lambda n: (n % 2, 0)),
            pl.BlockSpec((CH, EH * CZ), lambda n: (0, 0)),
        ],
        out_specs=pl.BlockSpec((2, HALF, 2 * CZ), lambda n: (n, 0, 0)),
        out_shape=jax.ShapeDtypeStruct((LOCAL, HALF, 2 * CZ), BF16),
        compiler_params=pltpu.CompilerParams(vmem_limit_bytes=16 * MIB),
        cost_estimate=pl.CostEstimate(flops=2 * 16 * S * CH * EH * CZ, bytes_accessed=9 * MIB, transcendentals=0),
        name="couple",
    )(theirs, mine, w)


def place8(own, core, t):
    rel = jnp.where((own + core) % 2 == 0, t - own, own - t) & 7
    half, low = rel >> 1, rel & 1
    return jnp.where(half == 0, low, jnp.where(half == 1, 4 + low, jnp.where(half == 2, 7 - low, 3 - low)))


def place4(own, core, t):
    rel = jnp.where((own + core) % 2 == 0, t - own, own - t) & 3
    return rel ^ (rel >> 1)


def holder4(own, core, k):
    step = (0, 1, -1, -2)[k]
    return (own + jnp.where((own + core) % 2 == 0, step, -step)) & 3


def half_kernel(count, *refs):
    r_refs, t_ref, o_ref = refs[:count], refs[count], refs[count + 1]
    for n in range(2):
        for k in range(count):
            o_ref[n, k * BLOCK // 2:(k + 1) * BLOCK // 2, :] = jnp.dot(
                r_refs[k][...], t_ref[n], preferred_element_type=F32)


def half(pieces, t):
    count = len(pieces)
    rows = count * BLOCK // 2
    return pl.pallas_call(
        lambda *refs: half_kernel(count, *refs),
        grid=(4,),
        in_specs=[pl.BlockSpec((BLOCK // 2, HALF), lambda n: (0, 0))] * count
        + [pl.BlockSpec((2, HALF, 2 * CZ), lambda n: (n, 0, 0))],
        out_specs=pl.BlockSpec((2, rows, 2 * CZ), lambda n: (n, 0, 0)),
        out_shape=jax.ShapeDtypeStruct((LOCAL, rows, 2 * CZ), F32),
        compiler_params=pltpu.CompilerParams(vmem_limit_bytes=24 * MIB),
        cost_estimate=pl.CostEstimate(flops=2 * rows * HALF * 2048, bytes_accessed=10 * MIB, transcendentals=0),
        name="half",
    )(*pieces, t)


def block_kernel(first, count, ready, at_ref, *refs):
    given = count if ready else 2 * count
    r_refs, refs = refs[:given], refs[given:]
    if ready:
        done_ref, refs = refs[0], refs[1:]
    t_ref, o_refs, sum_s, sem = refs[0], refs[1:-2], refs[-2], refs[-1]
    side_rows = BLOCK // 2
    copies = []
    if ready:
        pair = pl.ds((first + pl.program_id(0)) * 2, 2)
        for k in range(count):
            copies.append(pltpu.make_async_copy(
                done_ref.at[pair, pl.ds(k * side_rows, side_rows)], sum_s.at[:, pl.ds(k * BLOCK, side_rows)], sem.at[k]))
    for copy in copies:
        copy.start()
    core, z = at_ref[0], at_ref[3]
    minor = jnp.where(core == 0, at_ref[1], at_ref[2])
    pm = [place4(minor, core, t) for t in range(4)]
    pz = [place8(z, core, t) for t in range(8)]
    zrow = [(p >> 2) * side_rows + (p & 3) * UNIT for p in pz]
    for n in range(2):
        for k in range(given):
            row = k * BLOCK + side_rows if ready else k * side_rows
            sum_s[n, row:row + side_rows, :] = jnp.dot(r_refs[k][...], t_ref[n], preferred_element_type=F32)
    for copy in copies:
        copy.wait()

    def store(outs):
        for k in range(count):
            for n in range(2):
                for tm in range(4):
                    for c in range(2):
                        side = jnp.where(core == c, 0, LOCAL)
                        for tz in range(0, 8, 2):
                            both = []
                            for d in range(2):
                                row = zrow[tz + d] + pm[tm] * 4 * UNIT + side + k * BLOCK
                                both.append(sum_s[n, pl.ds(pl.multiple_of(row, LOCAL), LOCAL), :])
                            value = jnp.concatenate(both, axis=0).astype(BF16)
                            for i in range(2):
                                outs[k][n * 2 + i, tm, c, tz * LOCAL:(tz + 2) * LOCAL, :] = value[:, i * CZ:(i + 1) * CZ]

    if len(o_refs) == count:
        store(o_refs)
    else:
        pl.when(pl.program_id(0) < 2)(lambda: store(o_refs[:count]))
        pl.when(pl.program_id(0) >= 2)(lambda: store(o_refs[count:]))


def block(at, pieces, ready, t, part):
    count = len(pieces) // (2 if ready is None else 1)
    first = 2 if part == 1 else 0
    shape = (LOCAL, 4, 2, 64, CZ)
    spec = lambda where: pl.BlockSpec((4,) + shape[1:], lambda n, at: (where(n), 0, 0, 0, 0))
    if part is None:
        out_specs = [spec(lambda n: jnp.minimum(n, 1))] * count + [spec(lambda n: jnp.maximum(n - 2, 0))] * count
    else:
        out_specs = [spec(lambda n: n)] * count
    return pl.pallas_call(
        lambda *refs: block_kernel(first, count, ready is not None, *refs),
        grid_spec=pltpu.PrefetchScalarGridSpec(
            num_scalar_prefetch=1,
            grid=(4 if part is None else 2,),
            in_specs=[pl.BlockSpec((BLOCK // 2, HALF), lambda n, at: (0, 0))] * len(pieces)
            + ([] if ready is None else [pl.BlockSpec(memory_space=pl.ANY)])
            + [pl.BlockSpec((2, HALF, 2 * CZ), lambda n, at: (first + n, 0, 0))],
            out_specs=out_specs,
            scratch_shapes=[pltpu.VMEM((2, count * BLOCK, 2 * CZ), F32), pltpu.SemaphoreType.DMA((2,))],
        ),
        out_shape=[jax.ShapeDtypeStruct(shape, BF16)] * len(out_specs),
        compiler_params=pltpu.CompilerParams(vmem_limit_bytes=24 * MIB),
        cost_estimate=pl.CostEstimate(flops=BLOCK * len(pieces) * HALF * (2048 if part is None else 1024),
                                      bytes_accessed=10 * MIB, transcendentals=0),
        name="block",
    )(at, *pieces, *([] if ready is None else [ready]), t)


def add_kernel(at_ref, *refs):
    mine, theirs, bias_ref, o_ref = refs[0:4], refs[4:8], refs[8], refs[9]
    core = at_ref[0]
    minor = jnp.where(core == 0, at_ref[1], at_ref[2])
    major = jnp.where(core == 0, at_ref[2], at_ref[1])
    bias = bias_ref[...]
    for k in range(4):
        a = holder4(major, core, k)
        for m in range(4):
            b = holder4(minor, 1 - core, m)
            group = jnp.where(core == 0, b * 4 + a, a * 4 + b)
            for i in range(2):
                v = mine[k][i, b].astype(F32) + theirs[m][i, a].astype(F32)
                o_ref[i, group] = (v.reshape(128, CZ) + bias).astype(BF16).reshape(2, 64, CZ)


def add(at, mine, theirs, bias):
    return pl.pallas_call(
        add_kernel,
        grid_spec=pltpu.PrefetchScalarGridSpec(
            num_scalar_prefetch=1,
            grid=(LOCAL // 2,),
            in_specs=[pl.BlockSpec((2, 4, 2, 64, CZ), lambda n, at: (n, 0, 0, 0, 0))] * 8
            + [pl.BlockSpec((1, CZ), lambda n, at: (0, 0))],
            out_specs=pl.BlockSpec((2, 16, 2, 64, CZ), lambda n, at: (n, 0, 0, 0, 0)),
        ),
        out_shape=jax.ShapeDtypeStruct((LOCAL, 16, 2, 64, CZ), BF16),
        compiler_params=pltpu.CompilerParams(vmem_limit_bytes=24 * MIB),
        cost_estimate=pl.CostEstimate(flops=10**7, bytes_accessed=13 * MIB, transcendentals=0),
        name="add",
    )(at, *mine, *theirs, bias.reshape(1, CZ))


def partner(k, n, core, step):
    return (k + 1 if (k + core + step) % 2 == 0 else k - 1) % n


def along_z(v, step):
    return lax.ppermute(
        v, ("c", "z"), [(c * 8 + k, c * 8 + partner(k, 8, c, step)) for c in range(2) for k in range(8)])


def along_plane(v, last, step):
    pairs = []
    for y in range(4):
        for x in range(4):
            for c in range(2):
                ny, nx = (y, partner(x, 4, c, step)) if (c == 0) == last else (partner(y, 4, c, step), x)
                pairs.append(((y * 4 + x) * 2 + c, (ny * 4 + nx) * 2 + c))
    return lax.ppermute(v, ("y", "x", "c"), pairs)


def swap(v):
    return lax.ppermute(v, "c", [(0, 1), (1, 0)])


def join(*blocks):
    return jnp.concatenate(blocks, axis=0)


def together(*values):
    return lax.optimization_barrier(values)


def per_device(msa, gain, shift, w1, b1, w2, b2, couple_map, couple_offset):
    core = lax.axis_index("c")
    at = jnp.stack([core, lax.axis_index("y"), lax.axis_index("x"), lax.axis_index("z")]).astype(jnp.int32)
    keep, give, lt = project(at, msa, gain, shift, w1, b1, w2, b2)
    r = join(keep, swap(give))
    w = lax.dynamic_slice_in_dim(couple_map.reshape(CH, CH, CZ), core * EH, EH, axis=1).reshape(CH, EH * CZ)

    z1 = join(r, along_z(r, 0))
    z2 = along_z(z1, 1)
    h0 = join(z1, z2)
    z3 = along_z(z2, 2)
    m1_0 = along_plane(h0, False, 0)
    m2_0 = along_plane(h0, False, 1)
    z4, lt = together(along_z(z3, 3), lt)
    m3_0 = along_plane(m1_0, False, 1)
    h1, lt_sibling = together(join(z3, z4), swap(lt))
    t = couple(lt_sibling, lt, w)
    m1_1 = along_plane(h1, False, 0)
    m2_1 = along_plane(h1, False, 1)
    m1_1, t = together(m1_1, t)
    m3_1 = along_plane(m1_1, False, 1)
    b0_0 = join(h0, m1_0, m2_0, m3_0)
    b1_0 = along_plane(b0_0, True, 0)
    b2_0 = along_plane(b0_0, True, 1)
    b0_1 = join(h1, m1_1, m2_1, m3_1)
    b1_1 = along_plane(b0_1, True, 0)
    b2_1 = along_plane(b0_1, True, 1)
    p0, q0 = block(at, [b0_0, b0_1], None, t, None)
    b1_0, b2_0, p0, q0 = together(b1_0, b2_0, p0, q0)
    b3_0 = along_plane(b1_0, True, 1)
    d12 = half([b1_0, b2_0], t)
    b2_1, d12 = together(b2_1, d12)
    b3_1 = along_plane(b2_1, True, 0)
    p1, p2, q1, q2 = block(at, [b1_1, b2_1], d12, t, None)
    b3_0, p1 = together(b3_0, p1)
    d3 = half([b3_0], t)
    b3_1, d3 = together(b3_1, d3)
    p3, = block(at, [b3_1], d3, t, 0)
    q3, = block(at, [b3_1], d3, t, 1)
    theirs = [swap(p) for p in (p0, p1, p2, p3)]
    mine = [q0, q1, q2, q3]
    return add(at, mine, theirs, couple_offset).reshape(LOCAL, 16 * 2 * 64, CZ)


def solution(mesh):
    fine = Mesh(mesh.devices.reshape(4, 4, 2, 8), ("y", "x", "c", "z"))
    rows = ("y", "x", "c", "z")
    return jax.shard_map(
        per_device,
        mesh=fine,
        in_specs=(P(None, rows, None), P(), P(), P(), P(), P(), P(), P(), P()),
        out_specs=P(rows, None, None),
        check_vma=False,
    )
```

```python
import jax
import jax.numpy as jnp
from jax import lax
from jax.experimental import pallas as pl
from jax.experimental.pallas import tpu as pltpu
from jax.sharding import Mesh, PartitionSpec as P

S, CM, CH, CZ, LOCAL = 128, 256, 32, 128, 8
EH = CH // 2
HALF = EH * S
UNIT = 2 * LOCAL
BLOCK = 4 * 8 * UNIT
MIB = 1024 * 1024
BF16, F32 = jnp.bfloat16, jnp.float32


def project_kernel(core_ref, msa_in, gain_in, shift_in, w1_in, b1_in, w2_in, b2_in, keep_ref, give_ref, lt_ref,
                   msa_ref, gain_ref, shift_ref, w_s, b1_ref, b2_ref, y_s, r_s, sem):
    pairs = ((msa_in, msa_ref), (gain_in, gain_ref), (shift_in, shift_ref), (w1_in, w_s.at[pl.ds(0, CH)]),
             (w2_in, w_s.at[pl.ds(CH, CH)]), (b1_in, b1_ref), (b2_in, b2_ref))
    copies = [pltpu.make_async_copy(src, dst, sem.at[k]) for k, (src, dst) in enumerate(pairs)]
    for copy in copies:
        copy.start()
    for copy in copies:
        copy.wait()
    x = msa_ref[...].astype(F32).reshape(S * LOCAL, CM)
    mean = jnp.mean(x, axis=-1, keepdims=True)
    centered = x - mean
    variance = jnp.mean(centered * centered, axis=-1, keepdims=True)
    normed = (centered * lax.rsqrt(variance + 1e-05) * gain_ref[...] + shift_ref[...]).astype(BF16)
    y = lax.dot_general(normed, w_s[...], (((1,), (1,)), ((), ())), preferred_element_type=F32)
    bias = jnp.concatenate([b1_ref[...], b2_ref[...]], axis=1)
    y_s[:, 0:2 * CH] = (y + bias).astype(BF16).astype(F32)
    for j in range(LOCAL):
        t = y_s[pl.ds(j, S, stride=LOCAL), :].T
        lt_ref[j * CH:(j + 1) * CH, :] = (t[0:CH] * (1.0 / S)).astype(BF16)
        r_s[j * CH:(j + 1) * CH, :] = t[CH:2 * CH]
    core = core_ref[0]
    for e in range(EH):
        keep_ref[:, e * S:(e + 1) * S] = r_s[pl.ds(core * EH + e, LOCAL, stride=CH), :].astype(BF16)
        give_ref[:, e * S:(e + 1) * S] = r_s[pl.ds((1 - core) * EH + e, LOCAL, stride=CH), :].astype(BF16)


def project(core, msa, gain, shift, w1, b1, w2, b2):
    return pl.pallas_call(
        project_kernel,
        grid_spec=pltpu.PrefetchScalarGridSpec(
            num_scalar_prefetch=1,
            grid=(1,),
            in_specs=[pl.BlockSpec(memory_space=pl.ANY)] * 7,
            out_specs=[
                pl.BlockSpec((LOCAL, HALF), lambda n, core: (0, 0)),
                pl.BlockSpec((LOCAL, HALF), lambda n, core: (0, 0)),
                pl.BlockSpec((LOCAL * CH, S), lambda n, core: (0, 0)),
            ],
            scratch_shapes=[
                pltpu.VMEM((S, LOCAL, CM), BF16),
                pltpu.VMEM((1, CM), F32),
                pltpu.VMEM((1, CM), F32),
                pltpu.VMEM((2 * CH, CM), BF16),
                pltpu.VMEM((1, CH), F32),
                pltpu.VMEM((1, CH), F32),
                pltpu.VMEM((S * LOCAL, S), F32),
                pltpu.VMEM((LOCAL * CH, S), F32),
                pltpu.SemaphoreType.DMA((7,)),
            ],
        ),
        out_shape=[
            jax.ShapeDtypeStruct((LOCAL, HALF), BF16),
            jax.ShapeDtypeStruct((LOCAL, HALF), BF16),
            jax.ShapeDtypeStruct((LOCAL * CH, S), BF16),
        ],
        compiler_params=pltpu.CompilerParams(vmem_limit_bytes=60 * MIB),
        name="project",
    )(core, msa, gain.reshape(1, CM), shift.reshape(1, CM), w1.T, b1.reshape(1, CH), w2.T, b2.reshape(1, CH))


def couple_kernel(theirs_ref, mine_ref, w_ref, t_ref):
    lt = jnp.where(pl.program_id(0) < 2, theirs_ref[...], mine_ref[...])
    for n in range(2):
        for i in range(2):
            row = (n * 2 + i) * CH
            t = lax.dot_general(lt[row:row + CH, :], w_ref[...], (((0,), (0,)), ((), ())),
                                preferred_element_type=F32).astype(BF16)
            for e in range(EH):
                t_ref[n, e * S:(e + 1) * S, i * CZ:(i + 1) * CZ] = t[:, e * CZ:(e + 1) * CZ]


def couple(theirs, mine, w):
    return pl.pallas_call(
        couple_kernel,
        grid=(4,),
        in_specs=[
            pl.BlockSpec((4 * CH, S), lambda n: (n % 2, 0)),
            pl.BlockSpec((4 * CH, S), lambda n: (n % 2, 0)),
            pl.BlockSpec((CH, EH * CZ), lambda n: (0, 0)),
        ],
        out_specs=pl.BlockSpec((2, HALF, 2 * CZ), lambda n: (n, 0, 0)),
        out_shape=jax.ShapeDtypeStruct((LOCAL, HALF, 2 * CZ), BF16),
        compiler_params=pltpu.CompilerParams(vmem_limit_bytes=16 * MIB),
        cost_estimate=pl.CostEstimate(flops=2 * 16 * S * CH * EH * CZ, bytes_accessed=9 * MIB, transcendentals=0),
        name="couple",
    )(theirs, mine, w)


def place8(own, core, t):
    rel = jnp.where((own + core) % 2 == 0, t - own, own - t) & 7
    half, low = rel >> 1, rel & 1
    return jnp.where(half == 0, low, jnp.where(half == 1, 4 + low, jnp.where(half == 2, 7 - low, 3 - low)))


def place4(own, core, t):
    rel = jnp.where((own + core) % 2 == 0, t - own, own - t) & 3
    return rel ^ (rel >> 1)


def holder4(own, core, k):
    step = (0, 1, -1, -2)[k]
    return (own + jnp.where((own + core) % 2 == 0, step, -step)) & 3


def half_kernel(count, *refs):
    r_refs, t_ref, o_ref = refs[:count], refs[count], refs[count + 1]
    for n in range(2):
        for k in range(count):
            o_ref[n, k * BLOCK // 2:(k + 1) * BLOCK // 2, :] = jnp.dot(
                r_refs[k][...], t_ref[n], preferred_element_type=F32)


def half(pieces, t):
    count = len(pieces)
    rows = count * BLOCK // 2
    return pl.pallas_call(
        lambda *refs: half_kernel(count, *refs),
        grid=(4,),
        in_specs=[pl.BlockSpec((BLOCK // 2, HALF), lambda n: (0, 0))] * count
        + [pl.BlockSpec((2, HALF, 2 * CZ), lambda n: (n, 0, 0))],
        out_specs=pl.BlockSpec((2, rows, 2 * CZ), lambda n: (n, 0, 0)),
        out_shape=jax.ShapeDtypeStruct((LOCAL, rows, 2 * CZ), F32),
        compiler_params=pltpu.CompilerParams(vmem_limit_bytes=24 * MIB),
        cost_estimate=pl.CostEstimate(flops=2 * rows * HALF * 2048, bytes_accessed=10 * MIB, transcendentals=0),
        name="half",
    )(*pieces, t)


def block_kernel(first, count, ready, at_ref, *refs):
    given = count if ready else 2 * count
    r_refs, refs = refs[:given], refs[given:]
    if ready:
        done_ref, refs = refs[0], refs[1:]
    t_ref, o_refs, sum_s, sem = refs[0], refs[1:-2], refs[-2], refs[-1]
    side_rows = BLOCK // 2
    copies = []
    if ready:
        pair = pl.ds((first + pl.program_id(0)) * 2, 2)
        for k in range(count):
            copies.append(pltpu.make_async_copy(
                done_ref.at[pair, pl.ds(k * side_rows, side_rows)], sum_s.at[:, pl.ds(k * BLOCK, side_rows)], sem.at[k]))
    for copy in copies:
        copy.start()
    core, z = at_ref[0], at_ref[3]
    minor = jnp.where(core == 0, at_ref[1], at_ref[2])
    pm = [place4(minor, core, t) for t in range(4)]
    pz = [place8(z, core, t) for t in range(8)]
    zrow = [(p >> 2) * side_rows + (p & 3) * UNIT for p in pz]
    for n in range(2):
        for k in range(given):
            row = k * BLOCK + side_rows if ready else k * side_rows
            sum_s[n, row:row + side_rows, :] = jnp.dot(r_refs[k][...], t_ref[n], preferred_element_type=F32)
    for copy in copies:
        copy.wait()

    def store(outs):
        for k in range(count):
            for n in range(2):
                for tm in range(4):
                    for c in range(2):
                        side = jnp.where(core == c, 0, LOCAL)
                        for tz in range(0, 8, 2):
                            both = []
                            for d in range(2):
                                row = zrow[tz + d] + pm[tm] * 4 * UNIT + side + k * BLOCK
                                both.append(sum_s[n, pl.ds(pl.multiple_of(row, LOCAL), LOCAL), :])
                            value = jnp.concatenate(both, axis=0).astype(BF16)
                            for i in range(2):
                                outs[k][n * 2 + i, tm, c, tz * LOCAL:(tz + 2) * LOCAL, :] = value[:, i * CZ:(i + 1) * CZ]

    if len(o_refs) == count:
        store(o_refs)
    else:
        pl.when(pl.program_id(0) < 2)(lambda: store(o_refs[:count]))
        pl.when(pl.program_id(0) >= 2)(lambda: store(o_refs[count:]))


def block(at, pieces, ready, t, part):
    count = len(pieces) // (2 if ready is None else 1)
    first = 2 if part == 1 else 0
    shape = (LOCAL, 4, 2, 64, CZ)
    spec = lambda where: pl.BlockSpec((4,) + shape[1:], lambda n, at: (where(n), 0, 0, 0, 0))
    if part is None:
        out_specs = [spec(lambda n: jnp.minimum(n, 1))] * count + [spec(lambda n: jnp.maximum(n - 2, 0))] * count
    else:
        out_specs = [spec(lambda n: n)] * count
    return pl.pallas_call(
        lambda *refs: block_kernel(first, count, ready is not None, *refs),
        grid_spec=pltpu.PrefetchScalarGridSpec(
            num_scalar_prefetch=1,
            grid=(4 if part is None else 2,),
            in_specs=[pl.BlockSpec((BLOCK // 2, HALF), lambda n, at: (0, 0))] * len(pieces)
            + ([] if ready is None else [pl.BlockSpec(memory_space=pl.ANY)])
            + [pl.BlockSpec((2, HALF, 2 * CZ), lambda n, at: (first + n, 0, 0))],
            out_specs=out_specs,
            scratch_shapes=[pltpu.VMEM((2, count * BLOCK, 2 * CZ), F32), pltpu.SemaphoreType.DMA((2,))],
        ),
        out_shape=[jax.ShapeDtypeStruct(shape, BF16)] * len(out_specs),
        compiler_params=pltpu.CompilerParams(vmem_limit_bytes=24 * MIB),
        cost_estimate=pl.CostEstimate(flops=BLOCK * len(pieces) * HALF * (2048 if part is None else 1024),
                                      bytes_accessed=10 * MIB, transcendentals=0),
        name="block",
    )(at, *pieces, *([] if ready is None else [ready]), t)


def add_kernel(at_ref, *refs):
    mine, theirs, bias_ref, o_ref = refs[0:4], refs[4:8], refs[8], refs[9]
    core = at_ref[0]
    minor = jnp.where(core == 0, at_ref[1], at_ref[2])
    major = jnp.where(core == 0, at_ref[2], at_ref[1])
    bias = bias_ref[...]
    for k in range(4):
        a = holder4(major, core, k)
        for m in range(4):
            b = holder4(minor, 1 - core, m)
            group = jnp.where(core == 0, b * 4 + a, a * 4 + b)
            for i in range(2):
                v = mine[k][i, b].astype(F32) + theirs[m][i, a].astype(F32)
                o_ref[i, group] = (v.reshape(128, CZ) + bias).astype(BF16).reshape(2, 64, CZ)


def add(at, mine, theirs, bias):
    return pl.pallas_call(
        add_kernel,
        grid_spec=pltpu.PrefetchScalarGridSpec(
            num_scalar_prefetch=1,
            grid=(LOCAL // 2,),
            in_specs=[pl.BlockSpec((2, 4, 2, 64, CZ), lambda n, at: (n, 0, 0, 0, 0))] * 8
            + [pl.BlockSpec((1, CZ), lambda n, at: (0, 0))],
            out_specs=pl.BlockSpec((2, 16, 2, 64, CZ), lambda n, at: (n, 0, 0, 0, 0)),
        ),
        out_shape=jax.ShapeDtypeStruct((LOCAL, 16, 2, 64, CZ), BF16),
        compiler_params=pltpu.CompilerParams(vmem_limit_bytes=24 * MIB),
        cost_estimate=pl.CostEstimate(flops=10**7, bytes_accessed=13 * MIB, transcendentals=0),
        name="add",
    )(at, *mine, *theirs, bias.reshape(1, CZ))


def partner(k, n, core, step):
    if step == 2:
        return (k + 2) % n
    return (k + 1 if (k + core + step) % 2 == 0 else k - 1) % n


def along_z(v, step):
    return lax.ppermute(
        v, ("c", "z"), [(c * 8 + k, c * 8 + partner(k, 8, c, step)) for c in range(2) for k in range(8)])


def along_plane(v, last, step):
    pairs = []
    for y in range(4):
        for x in range(4):
            for c in range(2):
                ny, nx = (y, partner(x, 4, c, step)) if (c == 0) == last else (partner(y, 4, c, step), x)
                pairs.append(((y * 4 + x) * 2 + c, (ny * 4 + nx) * 2 + c))
    return lax.ppermute(v, ("y", "x", "c"), pairs)


def swap(v):
    return lax.ppermute(v, "c", [(0, 1), (1, 0)])


def join(*blocks):
    return jnp.concatenate(blocks, axis=0)


def together(*values):
    return lax.optimization_barrier(values)


def per_device(msa, gain, shift, w1, b1, w2, b2, couple_map, couple_offset):
    core = lax.axis_index("c")
    at = jnp.stack([core, lax.axis_index("y"), lax.axis_index("x"), lax.axis_index("z")]).astype(jnp.int32)
    keep, give, lt = project(at, msa, gain, shift, w1, b1, w2, b2)
    r = join(keep, swap(give))
    w = lax.dynamic_slice_in_dim(couple_map.reshape(CH, CH, CZ), core * EH, EH, axis=1).reshape(CH, EH * CZ)

    z1 = join(r, along_z(r, 0))
    z2 = along_z(z1, 1)
    h0 = join(z1, z2)
    t = couple(swap(lt), lt, w)
    z3, t = together(along_z(z2, 0), t)
    m1_0 = along_plane(h0, False, 0)
    m2_0 = along_plane(h0, False, 1)
    z4, offset = together(along_z(z3, 1), couple_offset)
    m3_0 = along_plane(m1_0, False, 1)
    h1, offset = together(join(z3, z4), swap(offset))
    m1_1 = along_plane(h1, False, 0)
    m2_1 = along_plane(h1, False, 1)
    m3_1 = along_plane(h1, False, 2)
    b0_0 = join(h0, m1_0, m2_0, m3_0)
    b1_0 = along_plane(b0_0, True, 0)
    b2_0 = along_plane(b0_0, True, 1)
    b0_1 = join(h1, m1_1, m2_1, m3_1)
    b1_1 = along_plane(b0_1, True, 0)
    b2_1 = along_plane(b0_1, True, 1)
    p0, q0 = block(at, [b0_0, b0_1], None, t, None)
    b1_0, b2_0, p0, q0 = together(b1_0, b2_0, p0, q0)
    b3_0 = along_plane(b1_0, True, 1)
    d12 = half([b1_0, b2_0], t)
    b2_1, d12 = together(b2_1, d12)
    b3_1 = along_plane(b2_1, True, 0)
    p1, p2, q1, q2 = block(at, [b1_1, b2_1], d12, t, None)
    b3_0, p1 = together(b3_0, p1)
    d3 = half([b3_0], t)
    b3_1, d3 = together(b3_1, d3)
    p3, = block(at, [b3_1], d3, t, 0)
    q3, = block(at, [b3_1], d3, t, 1)
    theirs = [swap(p) for p in (p0, p1, p2, p3)]
    mine = [q0, q1, q2, q3]
    return add(at, mine, theirs, offset).reshape(LOCAL, 16 * 2 * 64, CZ)


def solution(mesh):
    fine = Mesh(mesh.devices.reshape(4, 4, 2, 8), ("y", "x", "c", "z"))
    rows = ("y", "x", "c", "z")
    return jax.shard_map(
        per_device,
        mesh=fine,
        in_specs=(P(None, rows, None), P(), P(), P(), P(), P(), P(), P(), P()),
        out_specs=P(rows, None, None),
        check_vma=False,
    )
```

```python
import jax
import jax.numpy as jnp
from jax import lax
from jax.experimental import pallas as pl
from jax.experimental.pallas import tpu as pltpu
from jax.sharding import Mesh, PartitionSpec as P

S, CM, CH, CZ, LOCAL = 128, 256, 32, 128, 8
EH = CH // 2
HALF = EH * S
UNIT = 2 * LOCAL
BLOCK = 4 * 8 * UNIT
MIB = 1024 * 1024
BF16, F32 = jnp.bfloat16, jnp.float32


def project_kernel(core_ref, msa_in, gain_in, shift_in, w1_in, b1_in, w2_in, b2_in, keep_ref, give_ref, lt_ref,
                   msa_ref, gain_ref, shift_ref, w_s, b1_ref, b2_ref, y_s, r_s, sem):
    pairs = ((msa_in, msa_ref), (gain_in, gain_ref), (shift_in, shift_ref), (w1_in, w_s.at[pl.ds(0, CH)]),
             (w2_in, w_s.at[pl.ds(CH, CH)]), (b1_in, b1_ref), (b2_in, b2_ref))
    copies = [pltpu.make_async_copy(src, dst, sem.at[k]) for k, (src, dst) in enumerate(pairs)]
    for copy in copies:
        copy.start()
    for copy in copies:
        copy.wait()
    x = msa_ref[...].astype(F32).reshape(S * LOCAL, CM)
    mean = jnp.mean(x, axis=-1, keepdims=True)
    centered = x - mean
    variance = jnp.mean(centered * centered, axis=-1, keepdims=True)
    normed = (centered * lax.rsqrt(variance + 1e-05) * gain_ref[...] + shift_ref[...]).astype(BF16)
    y = lax.dot_general(normed, w_s[...], (((1,), (1,)), ((), ())), preferred_element_type=F32)
    bias = jnp.concatenate([b1_ref[...], b2_ref[...]], axis=1)
    y_s[:, 0:2 * CH] = (y + bias).astype(BF16).astype(F32)
    for j in range(LOCAL):
        t = y_s[pl.ds(j, S, stride=LOCAL), :].T
        lt_ref[j * CH:(j + 1) * CH, :] = (t[0:CH] * (1.0 / S)).astype(BF16)
        r_s[j * CH:(j + 1) * CH, :] = t[CH:2 * CH]
    core = core_ref[0]
    for e in range(EH):
        keep_ref[:, e * S:(e + 1) * S] = r_s[pl.ds(core * EH + e, LOCAL, stride=CH), :].astype(BF16)
        give_ref[:, e * S:(e + 1) * S] = r_s[pl.ds((1 - core) * EH + e, LOCAL, stride=CH), :].astype(BF16)


def project(core, msa, gain, shift, w1, b1, w2, b2):
    return pl.pallas_call(
        project_kernel,
        grid_spec=pltpu.PrefetchScalarGridSpec(
            num_scalar_prefetch=1,
            grid=(1,),
            in_specs=[pl.BlockSpec(memory_space=pl.ANY)] * 7,
            out_specs=[
                pl.BlockSpec((LOCAL, HALF), lambda n, core: (0, 0)),
                pl.BlockSpec((LOCAL, HALF), lambda n, core: (0, 0)),
                pl.BlockSpec((LOCAL * CH, S), lambda n, core: (0, 0)),
            ],
            scratch_shapes=[
                pltpu.VMEM((S, LOCAL, CM), BF16),
                pltpu.VMEM((1, CM), F32),
                pltpu.VMEM((1, CM), F32),
                pltpu.VMEM((2 * CH, CM), BF16),
                pltpu.VMEM((1, CH), F32),
                pltpu.VMEM((1, CH), F32),
                pltpu.VMEM((S * LOCAL, S), F32),
                pltpu.VMEM((LOCAL * CH, S), F32),
                pltpu.SemaphoreType.DMA((7,)),
            ],
        ),
        out_shape=[
            jax.ShapeDtypeStruct((LOCAL, HALF), BF16),
            jax.ShapeDtypeStruct((LOCAL, HALF), BF16),
            jax.ShapeDtypeStruct((LOCAL * CH, S), BF16),
        ],
        compiler_params=pltpu.CompilerParams(vmem_limit_bytes=60 * MIB),
        name="project",
    )(core, msa, gain.reshape(1, CM), shift.reshape(1, CM), w1.T, b1.reshape(1, CH), w2.T, b2.reshape(1, CH))


def couple_kernel(theirs_ref, mine_ref, w_ref, t_ref):
    lt = jnp.where(pl.program_id(0) < 2, theirs_ref[...], mine_ref[...])
    for n in range(2):
        for i in range(2):
            row = (n * 2 + i) * CH
            t = lax.dot_general(lt[row:row + CH, :], w_ref[...], (((0,), (0,)), ((), ())),
                                preferred_element_type=F32).astype(BF16)
            for e in range(EH):
                t_ref[n, e * S:(e + 1) * S, i * CZ:(i + 1) * CZ] = t[:, e * CZ:(e + 1) * CZ]


def couple(theirs, mine, w):
    return pl.pallas_call(
        couple_kernel,
        grid=(4,),
        in_specs=[
            pl.BlockSpec((4 * CH, S), lambda n: (n % 2, 0)),
            pl.BlockSpec((4 * CH, S), lambda n: (n % 2, 0)),
            pl.BlockSpec((CH, EH * CZ), lambda n: (0, 0)),
        ],
        out_specs=pl.BlockSpec((2, HALF, 2 * CZ), lambda n: (n, 0, 0)),
        out_shape=jax.ShapeDtypeStruct((LOCAL, HALF, 2 * CZ), BF16),
        compiler_params=pltpu.CompilerParams(vmem_limit_bytes=16 * MIB),
        cost_estimate=pl.CostEstimate(flops=2 * 16 * S * CH * EH * CZ, bytes_accessed=9 * MIB, transcendentals=0),
        name="couple",
    )(theirs, mine, w)


def place8(own, core, t):
    rel = jnp.where((own + core) % 2 == 0, t - own, own - t) & 7
    half, low = rel >> 1, rel & 1
    return jnp.where(half == 0, low, jnp.where(half == 1, 4 + low, jnp.where(half == 2, 6 + low, 3 - low)))


def place4(own, core, t):
    rel = jnp.where((own + core) % 2 == 0, t - own, own - t) & 3
    return rel ^ (rel >> 1)


def holder4(own, core, k):
    step = (0, 1, -1, -2)[k]
    return (own + jnp.where((own + core) % 2 == 0, step, -step)) & 3


def half_kernel(count, *refs):
    r_refs, t_ref, o_ref = refs[:count], refs[count], refs[count + 1]
    for n in range(2):
        for k in range(count):
            o_ref[n, k * BLOCK // 2:(k + 1) * BLOCK // 2, :] = jnp.dot(
                r_refs[k][...], t_ref[n], preferred_element_type=F32)


def half(pieces, t):
    count = len(pieces)
    rows = count * BLOCK // 2
    return pl.pallas_call(
        lambda *refs: half_kernel(count, *refs),
        grid=(4,),
        in_specs=[pl.BlockSpec((BLOCK // 2, HALF), lambda n: (0, 0))] * count
        + [pl.BlockSpec((2, HALF, 2 * CZ), lambda n: (n, 0, 0))],
        out_specs=pl.BlockSpec((2, rows, 2 * CZ), lambda n: (n, 0, 0)),
        out_shape=jax.ShapeDtypeStruct((LOCAL, rows, 2 * CZ), F32),
        compiler_params=pltpu.CompilerParams(vmem_limit_bytes=24 * MIB),
        cost_estimate=pl.CostEstimate(flops=2 * rows * HALF * 2048, bytes_accessed=10 * MIB, transcendentals=0),
        name="half",
    )(*pieces, t)


def block_kernel(first, count, ready, at_ref, *refs):
    given = count if ready else 2 * count
    r_refs, refs = refs[:given], refs[given:]
    if ready:
        done_ref, refs = refs[0], refs[1:]
    t_ref, o_refs, sum_s, sem = refs[0], refs[1:-2], refs[-2], refs[-1]
    side_rows = BLOCK // 2
    copies = []
    if ready:
        pair = pl.ds((first + pl.program_id(0)) * 2, 2)
        for k in range(count):
            copies.append(pltpu.make_async_copy(
                done_ref.at[pair, pl.ds(k * side_rows, side_rows)], sum_s.at[:, pl.ds(k * BLOCK, side_rows)], sem.at[k]))
    for copy in copies:
        copy.start()
    core, z = at_ref[0], at_ref[3]
    minor = jnp.where(core == 0, at_ref[1], at_ref[2])
    pm = [place4(minor, core, t) for t in range(4)]
    pz = [place8(z, core, t) for t in range(8)]
    zrow = [(p >> 2) * side_rows + (p & 3) * UNIT for p in pz]
    for n in range(2):
        for k in range(given):
            row = k * BLOCK + side_rows if ready else k * side_rows
            sum_s[n, row:row + side_rows, :] = jnp.dot(r_refs[k][...], t_ref[n], preferred_element_type=F32)
    for copy in copies:
        copy.wait()

    def store(outs):
        for k in range(count):
            for n in range(2):
                for tm in range(4):
                    for c in range(2):
                        side = jnp.where(core == c, 0, LOCAL)
                        for tz in range(0, 8, 2):
                            both = []
                            for d in range(2):
                                row = zrow[tz + d] + pm[tm] * 4 * UNIT + side + k * BLOCK
                                both.append(sum_s[n, pl.ds(pl.multiple_of(row, LOCAL), LOCAL), :])
                            value = jnp.concatenate(both, axis=0).astype(BF16)
                            for i in range(2):
                                outs[k][n * 2 + i, tm, c, tz * LOCAL:(tz + 2) * LOCAL, :] = value[:, i * CZ:(i + 1) * CZ]

    if len(o_refs) == count:
        store(o_refs)
    else:
        pl.when(pl.program_id(0) < 2)(lambda: store(o_refs[:count]))
        pl.when(pl.program_id(0) >= 2)(lambda: store(o_refs[count:]))


def block(at, pieces, ready, t, part):
    count = len(pieces) // (2 if ready is None else 1)
    first = 2 if part == 1 else 0
    shape = (LOCAL, 4, 2, 64, CZ)
    spec = lambda where: pl.BlockSpec((4,) + shape[1:], lambda n, at: (where(n), 0, 0, 0, 0))
    if part is None:
        out_specs = [spec(lambda n: jnp.minimum(n, 1))] * count + [spec(lambda n: jnp.maximum(n - 2, 0))] * count
    else:
        out_specs = [spec(lambda n: n)] * count
    return pl.pallas_call(
        lambda *refs: block_kernel(first, count, ready is not None, *refs),
        grid_spec=pltpu.PrefetchScalarGridSpec(
            num_scalar_prefetch=1,
            grid=(4 if part is None else 2,),
            in_specs=[pl.BlockSpec((BLOCK // 2, HALF), lambda n, at: (0, 0))] * len(pieces)
            + ([] if ready is None else [pl.BlockSpec(memory_space=pl.ANY)])
            + [pl.BlockSpec((2, HALF, 2 * CZ), lambda n, at: (first + n, 0, 0))],
            out_specs=out_specs,
            scratch_shapes=[pltpu.VMEM((2, count * BLOCK, 2 * CZ), F32), pltpu.SemaphoreType.DMA((2,))],
        ),
        out_shape=[jax.ShapeDtypeStruct(shape, BF16)] * len(out_specs),
        compiler_params=pltpu.CompilerParams(vmem_limit_bytes=24 * MIB),
        cost_estimate=pl.CostEstimate(flops=BLOCK * len(pieces) * HALF * (2048 if part is None else 1024),
                                      bytes_accessed=10 * MIB, transcendentals=0),
        name="block",
    )(at, *pieces, *([] if ready is None else [ready]), t)


def add_kernel(at_ref, *refs):
    mine, theirs, bias_ref, o_ref = refs[0:4], refs[4:8], refs[8], refs[9]
    core = at_ref[0]
    minor = jnp.where(core == 0, at_ref[1], at_ref[2])
    major = jnp.where(core == 0, at_ref[2], at_ref[1])
    bias = bias_ref[...]
    for k in range(4):
        a = holder4(major, core, k)
        for m in range(4):
            b = holder4(minor, 1 - core, m)
            group = jnp.where(core == 0, b * 4 + a, a * 4 + b)
            for i in range(2):
                v = mine[k][i, b].astype(F32) + theirs[m][i, a].astype(F32)
                o_ref[i, group] = (v.reshape(128, CZ) + bias).astype(BF16).reshape(2, 64, CZ)


def add(at, mine, theirs, bias):
    return pl.pallas_call(
        add_kernel,
        grid_spec=pltpu.PrefetchScalarGridSpec(
            num_scalar_prefetch=1,
            grid=(LOCAL // 2,),
            in_specs=[pl.BlockSpec((2, 4, 2, 64, CZ), lambda n, at: (n, 0, 0, 0, 0))] * 8
            + [pl.BlockSpec((1, CZ), lambda n, at: (0, 0))],
            out_specs=pl.BlockSpec((2, 16, 2, 64, CZ), lambda n, at: (n, 0, 0, 0, 0)),
        ),
        out_shape=jax.ShapeDtypeStruct((LOCAL, 16, 2, 64, CZ), BF16),
        compiler_params=pltpu.CompilerParams(vmem_limit_bytes=24 * MIB),
        cost_estimate=pl.CostEstimate(flops=10**7, bytes_accessed=13 * MIB, transcendentals=0),
        name="add",
    )(at, *mine, *theirs, bias.reshape(1, CZ))


def partner(k, n, core, step):
    if step == 2:
        return (k + 2) % n
    return (k + 1 if (k + core + step) % 2 == 0 else k - 1) % n


def along_z(v, step):
    pairs = []
    for c in range(2):
        for k in range(8):
            ahead = 1 if (k + c) % 2 == 0 else -1
            source = (k + (ahead, -ahead, 2 * ahead, 4)[step]) % 8
            pairs.append((c * 8 + source, c * 8 + k))
    return lax.ppermute(v, ("c", "z"), pairs)


def along_plane(v, last, step):
    pairs = []
    for y in range(4):
        for x in range(4):
            for c in range(2):
                ny, nx = (y, partner(x, 4, c, step)) if (c == 0) == last else (partner(y, 4, c, step), x)
                pairs.append(((y * 4 + x) * 2 + c, (ny * 4 + nx) * 2 + c))
    return lax.ppermute(v, ("y", "x", "c"), pairs)


def swap(v):
    return lax.ppermute(v, "c", [(0, 1), (1, 0)])


def join(*blocks):
    return jnp.concatenate(blocks, axis=0)


def together(*values):
    return lax.optimization_barrier(values)


def per_device(msa, gain, shift, w1, b1, w2, b2, couple_map, couple_offset):
    core = lax.axis_index("c")
    at = jnp.stack([core, lax.axis_index("y"), lax.axis_index("x"), lax.axis_index("z")]).astype(jnp.int32)
    keep, give, lt = project(at, msa, gain, shift, w1, b1, w2, b2)
    r = join(keep, swap(give))
    w = lax.dynamic_slice_in_dim(couple_map.reshape(CH, CH, CZ), core * EH, EH, axis=1).reshape(CH, EH * CZ)

    z1 = join(r, along_z(r, 0))
    z2 = along_z(z1, 1)
    h0 = join(z1, z2)
    h0, lt, lt_sibling = together(h0, lt, swap(lt))
    t = couple(lt_sibling, lt, w)
    z3 = along_z(z1, 2)
    m1_0 = along_plane(h0, False, 0)
    m2_0 = along_plane(h0, False, 1)
    m3_0 = along_plane(h0, False, 2)
    z3, t = together(z3, t)
    z4, offset, t = together(along_z(z1, 3), couple_offset, t)
    h1, offset = together(join(z3, z4), swap(offset))
    m1_1 = along_plane(h1, False, 0)
    m2_1 = along_plane(h1, False, 1)
    m3_1 = along_plane(h1, False, 2)
    b0_0 = join(h0, m1_0, m2_0, m3_0)
    b1_0 = along_plane(b0_0, True, 0)
    b2_0 = along_plane(b0_0, True, 1)
    b0_1 = join(h1, m1_1, m2_1, m3_1)
    b1_1 = along_plane(b0_1, True, 0)
    b2_1 = along_plane(b0_1, True, 1)
    p0, q0 = block(at, [b0_0, b0_1], None, t, None)
    b1_0, b2_0, p0, q0 = together(b1_0, b2_0, p0, q0)
    b3_0 = along_plane(b1_0, True, 1)
    d12 = half([b1_0, b2_0], t)
    b2_1, d12 = together(b2_1, d12)
    b3_1 = along_plane(b2_1, True, 0)
    p1, p2, q1, q2 = block(at, [b1_1, b2_1], d12, t, None)
    b3_0, p1 = together(b3_0, p1)
    d3 = half([b3_0], t)
    b3_1, d3 = together(b3_1, d3)
    p3, = block(at, [b3_1], d3, t, 0)
    q3, = block(at, [b3_1], d3, t, 1)
    theirs = [swap(p) for p in (p0, p1, p2, p3)]
    mine = [q0, q1, q2, q3]
    return add(at, mine, theirs, offset).reshape(LOCAL, 16 * 2 * 64, CZ)


def solution(mesh):
    fine = Mesh(mesh.devices.reshape(4, 4, 2, 8), ("y", "x", "c", "z"))
    rows = ("y", "x", "c", "z")
    return jax.shard_map(
        per_device,
        mesh=fine,
        in_specs=(P(None, rows, None), P(), P(), P(), P(), P(), P(), P(), P()),
        out_specs=P(rows, None, None),
        check_vma=False,
    )
```

```python
import jax
import jax.numpy as jnp
from jax import lax
from jax.experimental import pallas as pl
from jax.experimental.pallas import tpu as pltpu
from jax.sharding import Mesh, PartitionSpec as P

S, CM, CH, CZ, LOCAL = 128, 256, 32, 128, 8
EH = CH // 2
HALF = EH * S
UNIT = 2 * LOCAL
BLOCK = 4 * 8 * UNIT
MIB = 1024 * 1024
BF16, F32 = jnp.bfloat16, jnp.float32


def project_kernel(core_ref, msa_in, gain_in, shift_in, w1_in, b1_in, w2_in, b2_in, keep_ref, give_ref, lt_ref,
                   msa_ref, gain_ref, shift_ref, w_s, b1_ref, b2_ref, y_s, r_s, sem):
    pairs = ((msa_in, msa_ref), (gain_in, gain_ref), (shift_in, shift_ref), (w1_in, w_s.at[pl.ds(0, CH)]),
             (w2_in, w_s.at[pl.ds(CH, CH)]), (b1_in, b1_ref), (b2_in, b2_ref))
    copies = [pltpu.make_async_copy(src, dst, sem.at[k]) for k, (src, dst) in enumerate(pairs)]
    for copy in copies:
        copy.start()
    for copy in copies:
        copy.wait()
    x = msa_ref[...].astype(F32).reshape(S * LOCAL, CM)
    mean = jnp.mean(x, axis=-1, keepdims=True)
    centered = x - mean
    variance = jnp.mean(centered * centered, axis=-1, keepdims=True)
    normed = (centered * lax.rsqrt(variance + 1e-05) * gain_ref[...] + shift_ref[...]).astype(BF16)
    y = lax.dot_general(normed, w_s[...], (((1,), (1,)), ((), ())), preferred_element_type=F32)
    bias = jnp.concatenate([b1_ref[...], b2_ref[...]], axis=1)
    y_s[:, 0:2 * CH] = (y + bias).astype(BF16).astype(F32)
    for j in range(LOCAL):
        t = y_s[pl.ds(j, S, stride=LOCAL), :].T
        lt_ref[j * CH:(j + 1) * CH, :] = (t[0:CH] * (1.0 / S)).astype(BF16)
        r_s[j * CH:(j + 1) * CH, :] = t[CH:2 * CH]
    core = core_ref[0]
    for e in range(EH):
        keep_ref[:, e * S:(e + 1) * S] = r_s[pl.ds(core * EH + e, LOCAL, stride=CH), :].astype(BF16)
        give_ref[:, e * S:(e + 1) * S] = r_s[pl.ds((1 - core) * EH + e, LOCAL, stride=CH), :].astype(BF16)


def project(core, msa, gain, shift, w1, b1, w2, b2):
    return pl.pallas_call(
        project_kernel,
        grid_spec=pltpu.PrefetchScalarGridSpec(
            num_scalar_prefetch=1,
            grid=(1,),
            in_specs=[pl.BlockSpec(memory_space=pl.ANY)] * 7,
            out_specs=[
                pl.BlockSpec((LOCAL, HALF), lambda n, core: (0, 0)),
                pl.BlockSpec((LOCAL, HALF), lambda n, core: (0, 0)),
                pl.BlockSpec((LOCAL * CH, S), lambda n, core: (0, 0)),
            ],
            scratch_shapes=[
                pltpu.VMEM((S, LOCAL, CM), BF16),
                pltpu.VMEM((1, CM), F32),
                pltpu.VMEM((1, CM), F32),
                pltpu.VMEM((2 * CH, CM), BF16),
                pltpu.VMEM((1, CH), F32),
                pltpu.VMEM((1, CH), F32),
                pltpu.VMEM((S * LOCAL, S), F32),
                pltpu.VMEM((LOCAL * CH, S), F32),
                pltpu.SemaphoreType.DMA((7,)),
            ],
        ),
        out_shape=[
            jax.ShapeDtypeStruct((LOCAL, HALF), BF16),
            jax.ShapeDtypeStruct((LOCAL, HALF), BF16),
            jax.ShapeDtypeStruct((LOCAL * CH, S), BF16),
        ],
        compiler_params=pltpu.CompilerParams(vmem_limit_bytes=60 * MIB),
        name="project",
    )(core, msa, gain.reshape(1, CM), shift.reshape(1, CM), w1.T, b1.reshape(1, CH), w2.T, b2.reshape(1, CH))


def couple_kernel(theirs_ref, mine_ref, w_ref, t_ref):
    lt = jnp.where(pl.program_id(0) < 2, theirs_ref[...], mine_ref[...])
    for n in range(2):
        for i in range(2):
            row = (n * 2 + i) * CH
            t = lax.dot_general(lt[row:row + CH, :], w_ref[...], (((0,), (0,)), ((), ())),
                                preferred_element_type=F32).astype(BF16)
            for e in range(EH):
                t_ref[n, e * S:(e + 1) * S, i * CZ:(i + 1) * CZ] = t[:, e * CZ:(e + 1) * CZ]


def couple(theirs, mine, w):
    return pl.pallas_call(
        couple_kernel,
        grid=(4,),
        in_specs=[
            pl.BlockSpec((4 * CH, S), lambda n: (n % 2, 0)),
            pl.BlockSpec((4 * CH, S), lambda n: (n % 2, 0)),
            pl.BlockSpec((CH, EH * CZ), lambda n: (0, 0)),
        ],
        out_specs=pl.BlockSpec((2, HALF, 2 * CZ), lambda n: (n, 0, 0)),
        out_shape=jax.ShapeDtypeStruct((LOCAL, HALF, 2 * CZ), BF16),
        compiler_params=pltpu.CompilerParams(vmem_limit_bytes=16 * MIB),
        cost_estimate=pl.CostEstimate(flops=2 * 16 * S * CH * EH * CZ, bytes_accessed=9 * MIB, transcendentals=0),
        name="couple",
    )(theirs, mine, w)


def place8(own, core, t):
    rel = jnp.where((own + core) % 2 == 0, t - own, own - t) & 7
    half, low = rel >> 1, rel & 1
    return jnp.where(half == 0, low, jnp.where(half == 1, 4 + low, jnp.where(half == 2, 6 + low, 3 - low)))


def place4(own, core, t):
    rel = jnp.where((own + core) % 2 == 0, t - own, own - t) & 3
    return rel ^ (rel >> 1)


def holder4(own, core, k):
    step = (0, 1, -1, -2)[k]
    return (own + jnp.where((own + core) % 2 == 0, step, -step)) & 3


def half_kernel(count, *refs):
    r_refs, t_ref, o_ref = refs[:count], refs[count], refs[count + 1]
    for n in range(2):
        for k in range(count):
            o_ref[n, k * BLOCK // 2:(k + 1) * BLOCK // 2, :] = jnp.dot(
                r_refs[k][...], t_ref[n], preferred_element_type=F32)


def half(pieces, t):
    count = len(pieces)
    rows = count * BLOCK // 2
    return pl.pallas_call(
        lambda *refs: half_kernel(count, *refs),
        grid=(4,),
        in_specs=[pl.BlockSpec((BLOCK // 2, HALF), lambda n: (0, 0))] * count
        + [pl.BlockSpec((2, HALF, 2 * CZ), lambda n: (n, 0, 0))],
        out_specs=pl.BlockSpec((2, rows, 2 * CZ), lambda n: (n, 0, 0)),
        out_shape=jax.ShapeDtypeStruct((LOCAL, rows, 2 * CZ), F32),
        compiler_params=pltpu.CompilerParams(vmem_limit_bytes=24 * MIB),
        cost_estimate=pl.CostEstimate(flops=2 * rows * HALF * 2048, bytes_accessed=10 * MIB, transcendentals=0),
        name="half",
    )(*pieces, t)


def block_kernel(first, count, ready, at_ref, *refs):
    given = count if ready else 2 * count
    r_refs, refs = refs[:given], refs[given:]
    if ready:
        done_ref, refs = refs[0], refs[1:]
    t_ref, o_refs, sum_s, sem = refs[0], refs[1:-2], refs[-2], refs[-1]
    side_rows = BLOCK // 2
    copies = []
    if ready:
        pair = pl.ds((first + pl.program_id(0)) * 2, 2)
        for k in range(count):
            copies.append(pltpu.make_async_copy(
                done_ref.at[pair, pl.ds(k * side_rows, side_rows)], sum_s.at[:, pl.ds(k * BLOCK, side_rows)], sem.at[k]))
    for copy in copies:
        copy.start()
    core, z = at_ref[0], at_ref[3]
    minor = jnp.where(core == 0, at_ref[1], at_ref[2])
    pm = [place4(minor, core, t) for t in range(4)]
    pz = [place8(z, core, t) for t in range(8)]
    zrow = [(p >> 2) * side_rows + (p & 3) * UNIT for p in pz]
    for n in range(2):
        for k in range(given):
            row = k * BLOCK + side_rows if ready else k * side_rows
            sum_s[n, row:row + side_rows, :] = jnp.dot(r_refs[k][...], t_ref[n], preferred_element_type=F32)
    for copy in copies:
        copy.wait()

    def store(outs):
        for k in range(count):
            for n in range(2):
                for tm in range(4):
                    for c in range(2):
                        side = jnp.where(core == c, 0, LOCAL)
                        for tz in range(0, 8, 2):
                            both = []
                            for d in range(2):
                                row = zrow[tz + d] + pm[tm] * 4 * UNIT + side + k * BLOCK
                                both.append(sum_s[n, pl.ds(pl.multiple_of(row, LOCAL), LOCAL), :])
                            value = jnp.concatenate(both, axis=0).astype(BF16)
                            for i in range(2):
                                outs[k][n * 2 + i, tm, c, tz * LOCAL:(tz + 2) * LOCAL, :] = value[:, i * CZ:(i + 1) * CZ]

    if len(o_refs) == count:
        store(o_refs)
    else:
        pl.when(pl.program_id(0) < 2)(lambda: store(o_refs[:count]))
        pl.when(pl.program_id(0) >= 2)(lambda: store(o_refs[count:]))


def block(at, pieces, ready, t, part):
    count = len(pieces) // (2 if ready is None else 1)
    first = 2 if part == 1 else 0
    shape = (LOCAL, 4, 2, 64, CZ)
    spec = lambda where: pl.BlockSpec((4,) + shape[1:], lambda n, at: (where(n), 0, 0, 0, 0))
    if part is None:
        out_specs = [spec(lambda n: jnp.minimum(n, 1))] * count + [spec(lambda n: jnp.maximum(n - 2, 0))] * count
    else:
        out_specs = [spec(lambda n: n)] * count
    return pl.pallas_call(
        lambda *refs: block_kernel(first, count, ready is not None, *refs),
        grid_spec=pltpu.PrefetchScalarGridSpec(
            num_scalar_prefetch=1,
            grid=(4 if part is None else 2,),
            in_specs=[pl.BlockSpec((BLOCK // 2, HALF), lambda n, at: (0, 0))] * len(pieces)
            + ([] if ready is None else [pl.BlockSpec(memory_space=pl.ANY)])
            + [pl.BlockSpec((2, HALF, 2 * CZ), lambda n, at: (first + n, 0, 0))],
            out_specs=out_specs,
            scratch_shapes=[pltpu.VMEM((2, count * BLOCK, 2 * CZ), F32), pltpu.SemaphoreType.DMA((2,))],
        ),
        out_shape=[jax.ShapeDtypeStruct(shape, BF16)] * len(out_specs),
        compiler_params=pltpu.CompilerParams(vmem_limit_bytes=24 * MIB),
        cost_estimate=pl.CostEstimate(flops=BLOCK * len(pieces) * HALF * (2048 if part is None else 1024),
                                      bytes_accessed=10 * MIB, transcendentals=0),
        name="block",
    )(at, *pieces, *([] if ready is None else [ready]), t)


def add_kernel(at_ref, *refs):
    mine, theirs, bias_ref, o_ref = refs[0:4], refs[4:8], refs[8], refs[9]
    core = at_ref[0]
    minor = jnp.where(core == 0, at_ref[1], at_ref[2])
    major = jnp.where(core == 0, at_ref[2], at_ref[1])
    bias = bias_ref[...]
    for k in range(4):
        a = holder4(major, core, k)
        for m in range(4):
            b = holder4(minor, 1 - core, m)
            group = jnp.where(core == 0, b * 4 + a, a * 4 + b)
            for i in range(4):
                v = mine[k][i, b].astype(F32) + theirs[m][i, a].astype(F32)
                o_ref[i, group] = (v.reshape(128, CZ) + bias).astype(BF16).reshape(2, 64, CZ)


def add(at, mine, theirs, bias):
    return pl.pallas_call(
        add_kernel,
        grid_spec=pltpu.PrefetchScalarGridSpec(
            num_scalar_prefetch=1,
            grid=(2,),
            in_specs=[pl.BlockSpec((4, 4, 2, 64, CZ), lambda n, at: (n, 0, 0, 0, 0))] * 8
            + [pl.BlockSpec((1, CZ), lambda n, at: (0, 0))],
            out_specs=pl.BlockSpec((4, 16, 2, 64, CZ), lambda n, at: (n, 0, 0, 0, 0)),
        ),
        out_shape=jax.ShapeDtypeStruct((LOCAL, 16, 2, 64, CZ), BF16),
        compiler_params=pltpu.CompilerParams(vmem_limit_bytes=24 * MIB),
        cost_estimate=pl.CostEstimate(flops=10**7, bytes_accessed=13 * MIB, transcendentals=0),
        name="add",
    )(at, *mine, *theirs, bias.reshape(1, CZ))


def partner(k, n, core, step):
    if step == 2:
        return (k + 2) % n
    return (k + 1 if (k + core + step) % 2 == 0 else k - 1) % n


def along_z(v, step):
    pairs = []
    for c in range(2):
        for k in range(8):
            ahead = 1 if (k + c) % 2 == 0 else -1
            source = (k + (ahead, -ahead, 2 * ahead, 4)[step]) % 8
            pairs.append((c * 8 + source, c * 8 + k))
    return lax.ppermute(v, ("c", "z"), pairs)


def along_plane(v, last, step):
    pairs = []
    for y in range(4):
        for x in range(4):
            for c in range(2):
                ny, nx = (y, partner(x, 4, c, step)) if (c == 0) == last else (partner(y, 4, c, step), x)
                pairs.append(((y * 4 + x) * 2 + c, (ny * 4 + nx) * 2 + c))
    return lax.ppermute(v, ("y", "x", "c"), pairs)


def swap(v):
    return lax.ppermute(v, "c", [(0, 1), (1, 0)])


def join(*blocks):
    return jnp.concatenate(blocks, axis=0)


def together(*values):
    return lax.optimization_barrier(values)


def per_device(msa, gain, shift, w1, b1, w2, b2, couple_map, couple_offset):
    core = lax.axis_index("c")
    at = jnp.stack([core, lax.axis_index("y"), lax.axis_index("x"), lax.axis_index("z")]).astype(jnp.int32)
    keep, give, lt = project(at, msa, gain, shift, w1, b1, w2, b2)
    r = join(keep, swap(give))
    w = lax.dynamic_slice_in_dim(couple_map.reshape(CH, CH, CZ), core * EH, EH, axis=1).reshape(CH, EH * CZ)

    z1 = join(r, along_z(r, 0))
    z2 = along_z(z1, 1)
    h0 = join(z1, z2)
    h0, lt, lt_sibling = together(h0, lt, swap(lt))
    t = couple(lt_sibling, lt, w)
    z3 = along_z(z1, 2)
    m1_0 = along_plane(h0, False, 0)
    m2_0 = along_plane(h0, False, 1)
    m3_0 = along_plane(h0, False, 2)
    z3, t = together(z3, t)
    z4, offset, t = together(along_z(z1, 3), couple_offset, t)
    h1, offset = together(join(z3, z4), swap(offset))
    m1_1 = along_plane(h1, False, 0)
    m2_1 = along_plane(h1, False, 1)
    m3_1 = along_plane(h1, False, 2)
    b0_0 = join(h0, m1_0, m2_0, m3_0)
    b1_0 = along_plane(b0_0, True, 0)
    b2_0 = along_plane(b0_0, True, 1)
    b0_1 = join(h1, m1_1, m2_1, m3_1)
    b1_1 = along_plane(b0_1, True, 0)
    b2_1 = along_plane(b0_1, True, 1)
    p0, q0 = block(at, [b0_0, b0_1], None, t, None)
    b1_0, b2_0, p0, q0 = together(b1_0, b2_0, p0, q0)
    b3_0 = along_plane(b1_0, True, 1)
    d12 = half([b1_0, b2_0], t)
    b2_1, d12 = together(b2_1, d12)
    b3_1 = along_plane(b2_1, True, 0)
    p1, p2, q1, q2 = block(at, [b1_1, b2_1], d12, t, None)
    b3_0, p1 = together(b3_0, p1)
    d3 = half([b3_0], t)
    b3_1, d3 = together(b3_1, d3)
    p3, = block(at, [b3_1], d3, t, 0)
    q3, = block(at, [b3_1], d3, t, 1)
    theirs = [swap(p) for p in (p0, p1, p2, p3)]
    mine = [q0, q1, q2, q3]
    return add(at, mine, theirs, offset).reshape(LOCAL, 16 * 2 * 64, CZ)


def solution(mesh):
    fine = Mesh(mesh.devices.reshape(4, 4, 2, 8), ("y", "x", "c", "z"))
    rows = ("y", "x", "c", "z")
    return jax.shard_map(
        per_device,
        mesh=fine,
        in_specs=(P(None, rows, None), P(), P(), P(), P(), P(), P(), P(), P()),
        out_specs=P(rows, None, None),
        check_vma=False,
    )
```
